32 devices in a mesh: seq: 8 (over z, x), ch: 4 (over y, core).
Axes of the slice: x: 2, y: 2, z: 4, core: 2. Of those that a mesh axis runs over, the one named last changes fastest.
Arguments:
- bins_in: bfloat16 [8192, 1536], P('seq', 'ch'), may hold values from -6 to 6
- pre_scale: float32 [3, 1536], P(None, 'ch'), may hold values from 0.5 to 2
- pre_shift: float32 [3, 1536], P(None, 'ch'), may hold values from -1 to 1
- conv_weight: bfloat16 [3, 3, 1536, 1536], P(None, None, None, 'ch'), may hold values from -0.09375 to 0.09375
- conv_bias: float32 [3, 1536], P(None, 'ch'), may hold values from -0.5 to 0.5
Outputs:
- bins_out: bfloat16 [8192, 1536], P('seq', 'ch')
The draws below stay inside these ranges and needn't reach their ends.
All inputs are finite; a program needn't handle non-finite values.
Results may differ from the reference program's by a relative error of at most 0.015.
Values may be sent and summed in bfloat16 or wider, within the bound.
A program may use at most 64 MiB of HBM per device.

```python
import math
import jax
import jax.numpy as jnp

C = 1536
LAYERS = 3
FIRST_SPACING1 = 64
SECOND_SPACING2 = 512
THIRD_SPACING3 = 4096
BINS = 8192


def shard_levels(key, extent, split, least, top_value):
    def one(dim, parts):
        heights = jax.random.uniform(jax.random.fold_in(jax.random.fold_in(key, 6), dim), (parts,), jnp.float32, least / len(split), top_value / len(split))
        return jnp.repeat(jnp.exp(heights), extent[dim] // parts).reshape((-1,) + (1,) * (len(extent) - dim - 1))

    gain = one(*split[0])
    for cut in split[1:]:
        gain = gain * one(*cut)
    return gain


def centred(stream_key, dims, deviation, limit, cuts=(), dtype=jnp.bfloat16):
    drawn = jax.random.normal(stream_key, dims, jnp.float32) * deviation
    if len(cuts) > 0:
        drawn = shard_levels(stream_key, dims, cuts, -0.22, 0.18) * drawn
    return jnp.clip(drawn, min=-limit, max=limit).astype(dtype)


def setup_inputs(seed: int = 0) -> dict:
    keys = jax.random.split(jax.random.key(seed), 6)
    bins_in = centred(keys[0], (BINS, C), 1.0, 6.0, ((0, 8), (1, 4)))
    pre_scale = jnp.clip(jnp.exp(math.log(2.0) - 1.3862944 * jax.random.uniform(keys[1], (LAYERS, C), jnp.float32) ** shard_levels(keys[1], (LAYERS, C), ((1, 4),), -0.2, 0.2)), 0.5, 2.0)
    pre_shift = jnp.clip(jax.random.uniform(keys[2], (LAYERS, C), jnp.float32, -1.0, 1.0) * shard_levels(keys[2], (LAYERS, C), ((1, 4),), -0.4, 0.0), -1.0, 1.0)
    conv_weight = centred(keys[3], (LAYERS, 3, C, C), (3 * C) ** -0.5, 0.09375, ((3, 4),))
    conv_bias = jnp.clip(jax.random.uniform(keys[4], (LAYERS, C), jnp.float32, -0.5, 0.5) * shard_levels(keys[4], (LAYERS, C), ((1, 4),), -0.4, 0.0), -0.5, 0.5)
    return dict(bins_in=bins_in, pre_scale=pre_scale, pre_shift=pre_shift, conv_weight=conv_weight, conv_bias=conv_bias)


def reference(bins_in, pre_scale, pre_shift, conv_weight, conv_bias):
    layer_spacings = (FIRST_SPACING1, SECOND_SPACING2, THIRD_SPACING3)
    stream = bins_in
    for layer_index in range(LAYERS):
        dilation = layer_spacings[layer_index]
        activated = jax.nn.gelu(stream.astype(jnp.float32) * pre_scale[layer_index] + pre_shift[layer_index], approximate=False).astype(jnp.bfloat16)
        padded = jnp.pad(activated, ((dilation, dilation), (0, 0)))
        summed = jnp.zeros((BINS, C), jnp.float32)
        for kernel_tap_index in range(3):
            window = padded[kernel_tap_index * dilation: kernel_tap_index * dilation + BINS]
            summed = summed + jnp.dot(window, conv_weight[layer_index, kernel_tap_index], preferred_element_type=jnp.float32)
        stream = (stream.astype(jnp.float32) + summed + conv_bias[layer_index]).astype(jnp.bfloat16)
    return stream
```

```python
import functools

import jax
import jax.numpy as jnp
from jax import lax
from jax.experimental import pallas as pl
from jax.experimental.pallas import tpu as pltpu
from jax.sharding import PartitionSpec as P

LAYERS = 3
SPACINGS = (64, 512, 4096)
PIECES = 4
MESH = pl.DeviceIdType.MESH
INV_SQRT2 = 0.7071067811865476


def kernel(
    n, x_ref, scale_ref, shift_ref, w_hbm, bias_ref, out_ref,
    full, w, acc, part, up_out, down_out, low_in, high_in,
    w_sem, core_send, core_recv, y_send, y_recv, fwd_send, fwd_recv,
    up_send, up_recv, down_send, down_recv,
):
    rows, width = x_ref.shape
    piece = rows // PIECES
    s = lax.axis_index("seq")
    c = lax.axis_index("ch")
    core = c + 1 - 2 * lax.rem(c, 2)
    across = lax.rem(c + 2, 4)
    hops = [max(1, d // rows) for d in SPACINGS]
    rims = [min(d, rows) for d in SPACINGS]
    starts = [sum(rims[:l]) for l in range(LAYERS)]
    has_up = [s + h < n for h in hops]
    has_down = [s >= h for h in hops]

    def columns(index):
        return pl.ds(pl.multiple_of(index * width, width), width)

    def span(j):
        return pl.ds(j * piece, piece)

    barrier = pltpu.get_barrier_semaphore()
    pl.semaphore_signal(barrier, inc=1, device_id={"ch": core}, device_id_type=MESH)
    pl.semaphore_signal(barrier, inc=1, device_id={"ch": across}, device_id_type=MESH)
    greeted = sorted(set(hops))
    for h in greeted:
        @pl.when(s + h < n)
        def _():
            pl.semaphore_signal(barrier, inc=1, device_id={"seq": s + h}, device_id_type=MESH)

        @pl.when(s >= h)
        def _():
            pl.semaphore_signal(barrier, inc=1, device_id={"seq": s - h}, device_id_type=MESH)

    w_copies = [pltpu.make_async_copy(w_hbm.at[l], w.at[l], w_sem.at[l]) for l in range(LAYERS)]
    for copy in w_copies:
        copy.start()

    def activate(l, j, value):
        z = value * scale_ref[l : l + 1, :] + shift_ref[l : l + 1, :]
        gelu = 0.5 * z * (1.0 + lax.erf(z * INV_SQRT2))
        full[l, span(j), columns(c)] = gelu.astype(jnp.bfloat16)
        acc[span(j), :] = value + bias_ref[l : l + 1, :]

    def block(l, j, owner):
        return full.at[l, span(j), columns(owner)]

    def core_copy(l, j):
        ref = block(l, j, c)
        return pltpu.make_async_remote_copy(
            ref, ref, core_send.at[l, j], core_recv.at[l, j],
            device_id={"ch": core}, device_id_type=MESH)

    def y_copy(l, j):
        ref = block(l, j, c)
        return pltpu.make_async_remote_copy(
            ref, ref, y_send.at[l, j], y_recv.at[l, j],
            device_id={"ch": across}, device_id_type=MESH)

    def fwd_copy(l, j):
        ref = block(l, j, across)
        return pltpu.make_async_remote_copy(
            ref, ref, fwd_send.at[l, j], fwd_recv.at[l, j],
            device_id={"ch": core}, device_id_type=MESH)

    def send(l, j):
        y_copy(l, j).start()
        core_copy(l, j).start()

    def arrive(l, j):
        y_copy(l, j).wait_recv()
        fwd_copy(l, j).start()
        core_copy(l, j).wait_recv()
        fwd_copy(l, j).wait_recv()

    def rim_rows(l, p):
        size = min(piece, rims[l])
        return pl.ds(starts[l] + p * size, size)

    def up_copy(l, p):
        at = rim_rows(l, p)
        return pltpu.make_async_remote_copy(
            up_out.at[at, :], low_in.at[at, :], up_send.at[l, p], up_recv.at[l, p],
            device_id={"seq": s + hops[l]}, device_id_type=MESH)

    def down_copy(l, p):
        at = rim_rows(l, p)
        return pltpu.make_async_remote_copy(
            down_out.at[at, :], high_in.at[at, :], down_send.at[l, p], down_recv.at[l, p],
            device_id={"seq": s - hops[l]}, device_id_type=MESH)

    def send_up(l, p, value):
        @pl.when(has_up[l])
        def _():
            up_out[rim_rows(l, p), :] = value().astype(jnp.bfloat16)
            up_copy(l, p).start()

    def send_down(l, p, value):
        @pl.when(has_down[l])
        def _():
            down_out[rim_rows(l, p), :] = value().astype(jnp.bfloat16)
            down_copy(l, p).start()

    def take_low(l, p, at):
        @pl.when(has_down[l])
        def _():
            up_copy(l, p).wait_recv()
            acc[at, :] += low_in[rim_rows(l, p), :].astype(jnp.float32)

    def take_high(l, p, at):
        @pl.when(has_up[l])
        def _():
            down_copy(l, p).wait_recv()
            acc[at, :] += high_in[rim_rows(l, p), :].astype(jnp.float32)

    def product(l, j, k):
        return jnp.dot(full[l, span(j), :], w[l, k], preferred_element_type=jnp.float32)

    def step(l, j):
        arrive(l, j)
        d = SPACINGS[l]
        if d >= rows:
            send_up(l, j, lambda: product(l, j, 0))
            send_down(l, j, lambda: product(l, j, 2))
            acc[span(j), :] += product(l, j, 1)
            return

        @pl.loop(0, 3)
        def _(k):
            part[k] = product(l, j, k)

        first = j * piece
        inside = max(0, min(piece, rows - d - first))
        if inside < piece:
            send_up(l, (first + inside + d - rows) // piece, lambda: part[0, inside:piece])
        outside = max(0, min(piece, d - first))
        if outside > 0:
            send_down(l, first // piece if d > piece else 0, lambda: part[2, 0:outside])
        acc[span(j), :] += part[1]
        if inside > 0:
            acc[pl.ds(first + d, inside), :] += part[0, 0:inside]
        if outside < piece:
            acc[pl.ds(first + outside - d, piece - outside), :] += part[2, outside:piece]

    def finish(l, j):
        d = SPACINGS[l]
        first = j * piece
        size = min(piece, rims[l])
        if first < rims[l]:
            take_low(l, first // size, pl.ds(first, size))
        if first + piece > rows - rims[l]:
            at = max(first, rows - rims[l])
            take_high(l, (at - (rows - rims[l])) // size, pl.ds(at, size))
        value = acc[span(j), :].astype(jnp.bfloat16)
        if l == LAYERS - 1:
            out_ref[span(j), :] = value
        else:
            activate(l + 1, j, value.astype(jnp.float32))
            send(l + 1, j)

    activate(0, 3, x_ref[span(3), :].astype(jnp.float32))
    met = 2
    for h in greeted:
        met = met + (s + h < n).astype(jnp.int32) + (s >= h).astype(jnp.int32)
    pl.semaphore_wait(barrier, met)
    send(0, 3)
    for j in (0, 1, 2):
        activate(0, j, x_ref[span(j), :].astype(jnp.float32))
        send(0, j)

    w_copies[0].wait()
    step(0, 3)
    step(0, 0)
    step(0, 1)
    finish(0, 0)
    step(0, 2)
    finish(0, 2)
    finish(0, 1)
    finish(0, 3)

    w_copies[1].wait()
    step(1, 0)
    step(1, 2)
    finish(1, 2)
    step(1, 1)
    finish(1, 0)
    step(1, 3)
    finish(1, 3)
    finish(1, 1)

    w_copies[2].wait()
    for j in (2, 0, 3, 1):
        step(2, j)
    for j in (2, 0, 3, 1):
        finish(2, j)

    for l in range(LAYERS):
        for j in range(PIECES):
            y_copy(l, j).wait_send()
            core_copy(l, j).wait_send()
            fwd_copy(l, j).wait_send()
        for p in range(max(1, rims[l] // piece)):
            @pl.when(has_up[l])
            def _():
                up_copy(l, p).wait_send()

            @pl.when(has_down[l])
            def _():
                down_copy(l, p).wait_send()


def per_device(n, bins_in, pre_scale, pre_shift, conv_weight, conv_bias):
    rows, width = bins_in.shape
    depth = conv_weight.shape[2]
    rim_total = sum(min(d, rows) for d in SPACINGS)
    vmem = pl.BlockSpec(memory_space=pltpu.VMEM)
    pair = pltpu.SemaphoreType.DMA((LAYERS, PIECES))
    rim = pltpu.VMEM((rim_total, width), jnp.bfloat16)
    return pl.pallas_call(
        functools.partial(kernel, n),
        out_shape=jax.ShapeDtypeStruct((rows, width), jnp.bfloat16),
        in_specs=[vmem, vmem, vmem, pl.BlockSpec(memory_space=pl.ANY), vmem],
        out_specs=vmem,
        scratch_shapes=[
            pltpu.VMEM((LAYERS, rows, depth), jnp.bfloat16),
            pltpu.VMEM((LAYERS, 3, depth, width), jnp.bfloat16),
            pltpu.VMEM((rows, width), jnp.float32),
            pltpu.VMEM((3, rows // PIECES, width), jnp.float32),
            rim, rim, rim, rim,
            pltpu.SemaphoreType.DMA((LAYERS,)),
        ] + [pair] * 10,
        compiler_params=pltpu.CompilerParams(
            collective_id=0, has_side_effects=True, vmem_limit_bytes=56 * 1024 * 1024
        ),
        cost_estimate=pl.CostEstimate(
            flops=2 * rows * depth * width * 9, bytes_accessed=9 * 2 * depth * width,
            transcendentals=3 * rows * width),
    )(bins_in, pre_scale, pre_shift, conv_weight, conv_bias)


def solution(mesh):
    return jax.shard_map(
        functools.partial(per_device, mesh.shape["seq"]),
        mesh=mesh,
        in_specs=(
            P("seq", "ch"),
            P(None, "ch"),
            P(None, "ch"),
            P(None, None, None, "ch"),
            P(None, "ch"),
        ),
        out_specs=P("seq", "ch"),
        check_vma=False,
    )
```

```python
import functools

import jax
import jax.numpy as jnp
from jax import lax
from jax.experimental import pallas as pl
from jax.experimental.pallas import tpu as pltpu
from jax.sharding import PartitionSpec as P

LAYERS = 3
SPACINGS = (64, 512, 4096)
PIECES = 4
FAR_ORDER = (2, 0, 3, 1)
RAW = 3
MESH = pl.DeviceIdType.MESH
INV_SQRT2 = 0.7071067811865476


def kernel(
    n, x_ref, scale_ref, shift_ref, w_hbm, bias_ref, out_ref,
    full, w, acc, part, up_out, down_out, low_in, high_in, far,
    w_sem, core_send, core_recv, y_send, y_recv, fwd_send, fwd_recv,
    up_send, up_recv, down_send, down_recv,
    raw_send, raw_recv, far_core_send, far_core_recv, far_y_send, far_y_recv,
    far_fwd_send, far_fwd_recv,
):
    rows, width = x_ref.shape
    piece = rows // PIECES
    s = lax.axis_index("seq")
    c = lax.axis_index("ch")
    core = c + 1 - 2 * lax.rem(c, 2)
    across = lax.rem(c + 2, 4)
    hops = [max(1, d // rows) for d in SPACINGS]
    rims = [d if d < rows else piece for d in SPACINGS]
    starts = [sum(rims[:l]) for l in range(LAYERS)]
    has_up = [s + h < n for h in hops]
    has_down = [s >= h for h in hops]

    near = lax.div(c, 2)

    def chip(index):
        return pl.ds(pl.multiple_of(index * (2 * width), 2 * width), 2 * width)

    def dot(a, b):
        return jnp.dot(a, b, preferred_element_type=jnp.float32)

    def columns(index):
        return pl.ds(pl.multiple_of(index * width, width), width)

    def span(j):
        return pl.ds(j * piece, piece)

    barrier = pltpu.get_barrier_semaphore()
    pl.semaphore_signal(barrier, inc=1, device_id={"ch": core}, device_id_type=MESH)
    pl.semaphore_signal(barrier, inc=1, device_id={"ch": across}, device_id_type=MESH)
    greeted = sorted(set(hops))
    for h in greeted:
        @pl.when(s + h < n)
        def _():
            pl.semaphore_signal(barrier, inc=1, device_id={"seq": s + h}, device_id_type=MESH)

        @pl.when(s >= h)
        def _():
            pl.semaphore_signal(barrier, inc=1, device_id={"seq": s - h}, device_id_type=MESH)

    w_copies = [pltpu.make_async_copy(w_hbm.at[l], w.at[l], w_sem.at[l]) for l in range(LAYERS)]
    for copy in w_copies:
        copy.start()

    def activate(l, j, value):
        z = value * scale_ref[l : l + 1, :] + shift_ref[l : l + 1, :]
        gelu = 0.5 * z * (1.0 + lax.erf(z * INV_SQRT2))
        full[l, span(j), columns(c)] = gelu.astype(jnp.bfloat16)
        acc[span(j), :] = value + bias_ref[l : l + 1, :]

    def block(l, j, owner):
        return full.at[l, span(j), columns(owner)]

    def core_copy(l, j):
        ref = block(l, j, c)
        return pltpu.make_async_remote_copy(
            ref, ref, core_send.at[l, j], core_recv.at[l, j],
            device_id={"ch": core}, device_id_type=MESH)

    def y_copy(l, j):
        ref = block(l, j, c)
        return pltpu.make_async_remote_copy(
            ref, ref, y_send.at[l, j], y_recv.at[l, j],
            device_id={"ch": across}, device_id_type=MESH)

    def fwd_copy(l, j):
        ref = block(l, j, across)
        return pltpu.make_async_remote_copy(
            ref, ref, fwd_send.at[l, j], fwd_recv.at[l, j],
            device_id={"ch": core}, device_id_type=MESH)

    def send(l, j):
        y_copy(l, j).start()
        core_copy(l, j).start()

    def arrive(l, j):
        y_copy(l, j).wait_recv()
        fwd_copy(l, j).start()
        core_copy(l, j).wait_recv()

    last = LAYERS - 1
    far_on = (has_down[last], has_up[last])

    def raw_copy(side, p):
        to = s + hops[last] if side == 0 else s - hops[last]
        return pltpu.make_async_remote_copy(
            block(last, FAR_ORDER[p], c), far.at[side, span(p), columns(c)],
            raw_send.at[side, p], raw_recv.at[side, p],
            device_id={"seq": to}, device_id_type=MESH)

    def far_copy(side, p, owner, send_sem, recv_sem, to):
        ref = far.at[side, span(p), columns(owner)]
        return pltpu.make_async_remote_copy(
            ref, ref, send_sem.at[side, p], recv_sem.at[side, p],
            device_id={"ch": to}, device_id_type=MESH)

    def far_core(side, p):
        return far_copy(side, p, c, far_core_send, far_core_recv, core)

    def far_y(side, p):
        return far_copy(side, p, c, far_y_send, far_y_recv, across)

    def far_fwd(side, p):
        return far_copy(side, p, across, far_fwd_send, far_fwd_recv, core)

    def send_raw(p):
        for side, on in ((0, has_up[last]), (1, has_down[last])):
            @pl.when(on)
            def _():
                raw_copy(side, p).start()

    def relay(p):
        for side in range(2):
            @pl.when(far_on[side])
            def _():
                raw_copy(side, p).wait_recv()
                far_y(side, p).start()
                far_core(side, p).start()

    def add_far(p):
        for side in range(2):
            @pl.when(far_on[side])
            def _():
                far_y(side, p).wait_recv()
                far_fwd(side, p).start()
                far_core(side, p).wait_recv()
                at = span(FAR_ORDER[p])
                acc[at, :] += dot(far[side, span(p), chip(near)], w[last, 2 * side, chip(near), :])
                far_fwd(side, p).wait_recv()
                acc[at, :] += dot(far[side, span(p), chip(1 - near)], w[last, 2 * side, chip(1 - near), :])

    def rim_rows(l, p):
        size = min(piece, rims[l])
        return pl.ds(starts[l] + p * size, size)

    def up_copy(l, p):
        at = rim_rows(l, p)
        return pltpu.make_async_remote_copy(
            up_out.at[at, :], low_in.at[at, :], up_send.at[l, p], up_recv.at[l, p],
            device_id={"seq": s + hops[l]}, device_id_type=MESH)

    def down_copy(l, p):
        at = rim_rows(l, p)
        return pltpu.make_async_remote_copy(
            down_out.at[at, :], high_in.at[at, :], down_send.at[l, p], down_recv.at[l, p],
            device_id={"seq": s - hops[l]}, device_id_type=MESH)

    def send_up(l, p, value):
        @pl.when(has_up[l])
        def _():
            up_out[rim_rows(l, p), :] = value().astype(jnp.bfloat16)
            up_copy(l, p).start()

    def send_down(l, p, value):
        @pl.when(has_down[l])
        def _():
            down_out[rim_rows(l, p), :] = value().astype(jnp.bfloat16)
            down_copy(l, p).start()

    def take_low(l, p, at):
        @pl.when(has_down[l])
        def _():
            up_copy(l, p).wait_recv()
            acc[at, :] += low_in[rim_rows(l, p), :].astype(jnp.float32)

    def take_high(l, p, at):
        @pl.when(has_up[l])
        def _():
            down_copy(l, p).wait_recv()
            acc[at, :] += high_in[rim_rows(l, p), :].astype(jnp.float32)

    def product(l, j, k, index):
        return dot(full[l, span(j), chip(index)], w[l, k, chip(index), :])

    def step(l, j):
        arrive(l, j)
        d = SPACINGS[l]
        if d >= rows:
            acc[span(j), :] += product(l, j, 1, near)
            fwd_copy(l, j).wait_recv()
            if FAR_ORDER.index(j) >= RAW:
                send_up(l, 0, lambda: product(l, j, 0, near) + product(l, j, 0, 1 - near))
                send_down(l, 0, lambda: product(l, j, 2, near) + product(l, j, 2, 1 - near))
            acc[span(j), :] += product(l, j, 1, 1 - near)
            return

        @pl.loop(0, 3)
        def _(k):
            part[k] = product(l, j, k, near)

        fwd_copy(l, j).wait_recv()

        @pl.loop(0, 3)
        def _(k):
            part[k] += product(l, j, k, 1 - near)

        first = j * piece
        inside = max(0, min(piece, rows - d - first))
        if inside < piece:
            send_up(l, (first + inside + d - rows) // piece, lambda: part[0, inside:piece])
        outside = max(0, min(piece, d - first))
        if outside > 0:
            send_down(l, first // piece if d > piece else 0, lambda: part[2, 0:outside])
        acc[span(j), :] += part[1]
        if inside > 0:
            acc[pl.ds(first + d, inside), :] += part[0, 0:inside]
        if outside < piece:
            acc[pl.ds(first + outside - d, piece - outside), :] += part[2, outside:piece]

    def finish(l, j):
        first = j * piece
        size = min(piece, rims[l])
        if l == last:
            if FAR_ORDER.index(j) >= RAW:
                take_low(l, 0, span(j))
                take_high(l, 0, span(j))
            out_ref[span(j), :] = acc[span(j), :].astype(jnp.bfloat16)
            return
        if first < rims[l]:
            take_low(l, first // size, pl.ds(first, size))
        if first + piece > rows - rims[l]:
            at = max(first, rows - rims[l])
            take_high(l, (at - (rows - rims[l])) // size, pl.ds(at, size))
        value = acc[span(j), :].astype(jnp.bfloat16)
        activate(l + 1, j, value.astype(jnp.float32))
        if l + 1 == last and FAR_ORDER.index(j) < RAW:
            send_raw(FAR_ORDER.index(j))
        send(l + 1, j)

    activate(0, 3, x_ref[span(3), :].astype(jnp.float32))
    met = 2
    for h in greeted:
        met = met + (s + h < n).astype(jnp.int32) + (s >= h).astype(jnp.int32)
    pl.semaphore_wait(barrier, met)
    send(0, 3)
    for j in (0, 1, 2):
        activate(0, j, x_ref[span(j), :].astype(jnp.float32))
        send(0, j)

    w_copies[0].wait()
    step(0, 3)
    step(0, 0)
    step(0, 1)
    finish(0, 0)
    step(0, 2)
    finish(0, 2)
    finish(0, 1)
    finish(0, 3)

    w_copies[1].wait()
    step(1, 0)
    step(1, 2)
    finish(1, 2)
    step(1, 1)
    finish(1, 0)
    step(1, 3)
    finish(1, 3)
    finish(1, 1)

    w_copies[2].wait()
    step(2, 2)
    relay(0)
    step(2, 0)
    step(2, 3)
    relay(1)
    step(2, 1)
    add_far(0)
    finish(2, 2)
    relay(2)
    add_far(1)
    finish(2, 0)
    add_far(2)
    finish(2, 3)
    finish(2, 1)

    for p in range(RAW):
        for side, on in ((0, has_up[last]), (1, has_down[last])):
            @pl.when(on)
            def _():
                raw_copy(side, p).wait_send()

            @pl.when(far_on[side])
            def _():
                far_y(side, p).wait_send()
                far_core(side, p).wait_send()
                far_fwd(side, p).wait_send()
    for l in range(LAYERS):
        for j in range(PIECES):
            y_copy(l, j).wait_send()
            core_copy(l, j).wait_send()
            fwd_copy(l, j).wait_send()
        for p in range(max(1, rims[l] // piece)):
            @pl.when(has_up[l])
            def _():
                up_copy(l, p).wait_send()

            @pl.when(has_down[l])
            def _():
                down_copy(l, p).wait_send()


def per_device(n, bins_in, pre_scale, pre_shift, conv_weight, conv_bias):
    rows, width = bins_in.shape
    depth = conv_weight.shape[2]
    rim_total = sum(d if d < rows else rows // PIECES for d in SPACINGS)
    vmem = pl.BlockSpec(memory_space=pltpu.VMEM)
    pair = pltpu.SemaphoreType.DMA((LAYERS, PIECES))
    rim = pltpu.VMEM((rim_total, width), jnp.bfloat16)
    return pl.pallas_call(
        functools.partial(kernel, n),
        out_shape=jax.ShapeDtypeStruct((rows, width), jnp.bfloat16),
        in_specs=[vmem, vmem, vmem, pl.BlockSpec(memory_space=pl.ANY), vmem],
        out_specs=vmem,
        scratch_shapes=[
            pltpu.VMEM((LAYERS, rows, depth), jnp.bfloat16),
            pltpu.VMEM((LAYERS, 3, depth, width), jnp.bfloat16),
            pltpu.VMEM((rows, width), jnp.float32),
            pltpu.VMEM((3, rows // PIECES, width), jnp.float32),
            rim, rim, rim, rim,
            pltpu.VMEM((2, RAW * rows // PIECES, depth), jnp.bfloat16),
            pltpu.SemaphoreType.DMA((LAYERS,)),
        ] + [pair] * 10 + [pltpu.SemaphoreType.DMA((2, RAW))] * 8,
        compiler_params=pltpu.CompilerParams(
            collective_id=0, has_side_effects=True, vmem_limit_bytes=56 * 1024 * 1024
        ),
        cost_estimate=pl.CostEstimate(
            flops=2 * rows * depth * width * 9, bytes_accessed=9 * 2 * depth * width,
            transcendentals=3 * rows * width),
    )(bins_in, pre_scale, pre_shift, conv_weight, conv_bias)


def solution(mesh):
    return jax.shard_map(
        functools.partial(per_device, mesh.shape["seq"]),
        mesh=mesh,
        in_specs=(
            P("seq", "ch"),
            P(None, "ch"),
            P(None, "ch"),
            P(None, None, None, "ch"),
            P(None, "ch"),
        ),
        out_specs=P("seq", "ch"),
        check_vma=False,
    )
```

```python
import functools

import jax
import jax.numpy as jnp
from jax import lax
from jax.experimental import pallas as pl
from jax.experimental.pallas import tpu as pltpu
from jax.sharding import PartitionSpec as P

LAYERS = 3
SPACINGS = (64, 512, 4096)
PIECES = 4
FAR_ORDER = (2, 0, 3, 1)
RAW = 2
MESH = pl.DeviceIdType.MESH
INV_SQRT2 = 0.7071067811865476


def kernel(
    n, x_ref, scale_ref, shift_ref, w_hbm, bias_ref, out_ref,
    full, w, acc, part, up_out, down_out, low_in, high_in, far,
    w_sem, core_send, core_recv, y_send, y_recv, fwd_send, fwd_recv,
    up_send, up_recv, down_send, down_recv,
    raw_send, raw_recv, far_core_send, far_core_recv, far_y_send, far_y_recv,
    far_fwd_send, far_fwd_recv,
):
    rows, width = x_ref.shape
    piece = rows // PIECES
    s = lax.axis_index("seq")
    c = lax.axis_index("ch")
    core = c + 1 - 2 * lax.rem(c, 2)
    across = lax.rem(c + 2, 4)
    hops = [max(1, d // rows) for d in SPACINGS]
    rims = [d if d < rows else (PIECES - RAW) * piece for d in SPACINGS]
    starts = [sum(rims[:l]) for l in range(LAYERS)]
    has_up = [s + h < n for h in hops]
    has_down = [s >= h for h in hops]

    def dot(a, b):
        return jnp.dot(a, b, preferred_element_type=jnp.float32)

    def columns(index):
        return pl.ds(pl.multiple_of(index * width, width), width)

    def span(j):
        return pl.ds(j * piece, piece)

    barrier = pltpu.get_barrier_semaphore()
    pl.semaphore_signal(barrier, inc=1, device_id={"ch": core}, device_id_type=MESH)
    pl.semaphore_signal(barrier, inc=1, device_id={"ch": across}, device_id_type=MESH)
    greeted = sorted(set(hops))
    for h in greeted:
        @pl.when(s + h < n)
        def _():
            pl.semaphore_signal(barrier, inc=1, device_id={"seq": s + h}, device_id_type=MESH)

        @pl.when(s >= h)
        def _():
            pl.semaphore_signal(barrier, inc=1, device_id={"seq": s - h}, device_id_type=MESH)

    w_copies = [pltpu.make_async_copy(w_hbm.at[l], w.at[l], w_sem.at[l]) for l in range(LAYERS)]
    for copy in w_copies:
        copy.start()

    def activate(l, j, value):
        z = value * scale_ref[l : l + 1, :] + shift_ref[l : l + 1, :]
        gelu = 0.5 * z * (1.0 + lax.erf(z * INV_SQRT2))
        full[l, span(j), columns(c)] = gelu.astype(jnp.bfloat16)
        acc[span(j), :] = value + bias_ref[l : l + 1, :]

    def block(l, j, owner):
        return full.at[l, span(j), columns(owner)]

    def core_copy(l, j):
        ref = block(l, j, c)
        return pltpu.make_async_remote_copy(
            ref, ref, core_send.at[l, j], core_recv.at[l, j],
            device_id={"ch": core}, device_id_type=MESH)

    def y_copy(l, j):
        ref = block(l, j, c)
        return pltpu.make_async_remote_copy(
            ref, ref, y_send.at[l, j], y_recv.at[l, j],
            device_id={"ch": across}, device_id_type=MESH)

    def fwd_copy(l, j):
        ref = block(l, j, across)
        return pltpu.make_async_remote_copy(
            ref, ref, fwd_send.at[l, j], fwd_recv.at[l, j],
            device_id={"ch": core}, device_id_type=MESH)

    def send(l, j):
        y_copy(l, j).start()
        core_copy(l, j).start()

    def arrive(l, j):
        y_copy(l, j).wait_recv()
        fwd_copy(l, j).start()
        core_copy(l, j).wait_recv()
        fwd_copy(l, j).wait_recv()

    last = LAYERS - 1
    far_on = (has_down[last], has_up[last])

    def raw_copy(side, p):
        to = s + hops[last] if side == 0 else s - hops[last]
        return pltpu.make_async_remote_copy(
            block(last, FAR_ORDER[p], c), far.at[side, span(p), columns(c)],
            raw_send.at[side, p], raw_recv.at[side, p],
            device_id={"seq": to}, device_id_type=MESH)

    def far_copy(side, p, owner, send_sem, recv_sem, to):
        ref = far.at[side, span(p), columns(owner)]
        return pltpu.make_async_remote_copy(
            ref, ref, send_sem.at[side, p], recv_sem.at[side, p],
            device_id={"ch": to}, device_id_type=MESH)

    def far_core(side, p):
        return far_copy(side, p, c, far_core_send, far_core_recv, core)

    def far_y(side, p):
        return far_copy(side, p, c, far_y_send, far_y_recv, across)

    def far_fwd(side, p):
        return far_copy(side, p, across, far_fwd_send, far_fwd_recv, core)

    def send_raw(p):
        for side, on in ((0, has_up[last]), (1, has_down[last])):
            @pl.when(on)
            def _():
                raw_copy(side, p).start()

    def relay(p):
        for side in range(2):
            @pl.when(far_on[side])
            def _():
                raw_copy(side, p).wait_recv()
                far_y(side, p).start()
                far_core(side, p).start()

    def add_far(p):
        for side in range(2):
            @pl.when(far_on[side])
            def _():
                far_y(side, p).wait_recv()
                far_fwd(side, p).start()
                far_core(side, p).wait_recv()
                far_fwd(side, p).wait_recv()
                acc[span(FAR_ORDER[p]), :] += dot(far[side, span(p), :], w[last, 2 * side])

    def rim_rows(l, p):
        size = min(piece, rims[l])
        return pl.ds(starts[l] + p * size, size)

    def up_copy(l, p):
        at = rim_rows(l, p)
        return pltpu.make_async_remote_copy(
            up_out.at[at, :], low_in.at[at, :], up_send.at[l, p], up_recv.at[l, p],
            device_id={"seq": s + hops[l]}, device_id_type=MESH)

    def down_copy(l, p):
        at = rim_rows(l, p)
        return pltpu.make_async_remote_copy(
            down_out.at[at, :], high_in.at[at, :], down_send.at[l, p], down_recv.at[l, p],
            device_id={"seq": s - hops[l]}, device_id_type=MESH)

    def send_up(l, p, value):
        @pl.when(has_up[l])
        def _():
            up_out[rim_rows(l, p), :] = value().astype(jnp.bfloat16)
            up_copy(l, p).start()

    def send_down(l, p, value):
        @pl.when(has_down[l])
        def _():
            down_out[rim_rows(l, p), :] = value().astype(jnp.bfloat16)
            down_copy(l, p).start()

    def take_low(l, p, at):
        @pl.when(has_down[l])
        def _():
            up_copy(l, p).wait_recv()
            acc[at, :] += low_in[rim_rows(l, p), :].astype(jnp.float32)

    def take_high(l, p, at):
        @pl.when(has_up[l])
        def _():
            down_copy(l, p).wait_recv()
            acc[at, :] += high_in[rim_rows(l, p), :].astype(jnp.float32)

    def product(l, j, k):
        return dot(full[l, span(j), :], w[l, k])

    def step(l, j):
        arrive(l, j)
        d = SPACINGS[l]
        if d >= rows:
            p = FAR_ORDER.index(j) - RAW
            if p >= 0:
                send_up(l, p, lambda: product(l, j, 0))
                send_down(l, p, lambda: product(l, j, 2))
            acc[span(j), :] += product(l, j, 1)
            return

        @pl.loop(0, 3)
        def _(k):
            part[k] = product(l, j, k)

        first = j * piece
        inside = max(0, min(piece, rows - d - first))
        if inside < piece:
            send_up(l, (first + inside + d - rows) // piece, lambda: part[0, inside:piece])
        outside = max(0, min(piece, d - first))
        if outside > 0:
            send_down(l, first // piece if d > piece else 0, lambda: part[2, 0:outside])
        acc[span(j), :] += part[1]
        if inside > 0:
            acc[pl.ds(first + d, inside), :] += part[0, 0:inside]
        if outside < piece:
            acc[pl.ds(first + outside - d, piece - outside), :] += part[2, outside:piece]

    def finish(l, j):
        first = j * piece
        size = min(piece, rims[l])
        if l == last:
            p = FAR_ORDER.index(j) - RAW
            if p >= 0:
                take_low(l, p, span(j))
                take_high(l, p, span(j))
            out_ref[span(j), :] = acc[span(j), :].astype(jnp.bfloat16)
            return
        if first < rims[l]:
            take_low(l, first // size, pl.ds(first, size))
        if first + piece > rows - rims[l]:
            at = max(first, rows - rims[l])
            take_high(l, (at - (rows - rims[l])) // size, pl.ds(at, size))
        value = acc[span(j), :].astype(jnp.bfloat16)
        activate(l + 1, j, value.astype(jnp.float32))
        if l + 1 == last and FAR_ORDER.index(j) < RAW:
            send_raw(FAR_ORDER.index(j))
        send(l + 1, j)

    activate(0, 3, x_ref[span(3), :].astype(jnp.float32))
    met = 2
    for h in greeted:
        met = met + (s + h < n).astype(jnp.int32) + (s >= h).astype(jnp.int32)
    pl.semaphore_wait(barrier, met)
    send(0, 3)
    for j in (0, 1, 2):
        activate(0, j, x_ref[span(j), :].astype(jnp.float32))
        send(0, j)

    w_copies[0].wait()
    step(0, 3)
    step(0, 0)
    step(0, 1)
    finish(0, 0)
    step(0, 2)
    finish(0, 2)
    finish(0, 1)
    finish(0, 3)

    w_copies[1].wait()
    step(1, 0)
    step(1, 2)
    finish(1, 2)
    step(1, 1)
    finish(1, 0)
    step(1, 3)
    finish(1, 3)
    finish(1, 1)

    w_copies[2].wait()
    step(2, 2)
    step(2, 0)
    step(2, 3)
    relay(0)
    step(2, 1)
    relay(1)
    add_far(0)
    finish(2, 2)
    add_far(1)
    finish(2, 0)
    finish(2, 3)
    finish(2, 1)

    for p in range(RAW):
        for side, on in ((0, has_up[last]), (1, has_down[last])):
            @pl.when(on)
            def _():
                raw_copy(side, p).wait_send()

            @pl.when(far_on[side])
            def _():
                far_y(side, p).wait_send()
                far_core(side, p).wait_send()
                far_fwd(side, p).wait_send()
    for l in range(LAYERS):
        for j in range(PIECES):
            y_copy(l, j).wait_send()
            core_copy(l, j).wait_send()
            fwd_copy(l, j).wait_send()
        for p in range(max(1, rims[l] // piece)):
            @pl.when(has_up[l])
            def _():
                up_copy(l, p).wait_send()

            @pl.when(has_down[l])
            def _():
                down_copy(l, p).wait_send()


def per_device(n, bins_in, pre_scale, pre_shift, conv_weight, conv_bias):
    rows, width = bins_in.shape
    depth = conv_weight.shape[2]
    rim_total = sum(d if d < rows else (PIECES - RAW) * rows // PIECES for d in SPACINGS)
    vmem = pl.BlockSpec(memory_space=pltpu.VMEM)
    pair = pltpu.SemaphoreType.DMA((LAYERS, PIECES))
    rim = pltpu.VMEM((rim_total, width), jnp.bfloat16)
    return pl.pallas_call(
        functools.partial(kernel, n),
        out_shape=jax.ShapeDtypeStruct((rows, width), jnp.bfloat16),
        in_specs=[vmem, vmem, vmem, pl.BlockSpec(memory_space=pl.ANY), vmem],
        out_specs=vmem,
        scratch_shapes=[
            pltpu.VMEM((LAYERS, rows, depth), jnp.bfloat16),
            pltpu.VMEM((LAYERS, 3, depth, width), jnp.bfloat16),
            pltpu.VMEM((rows, width), jnp.float32),
            pltpu.VMEM((3, rows // PIECES, width), jnp.float32),
            rim, rim, rim, rim,
            pltpu.VMEM((2, RAW * rows // PIECES, depth), jnp.bfloat16),
            pltpu.SemaphoreType.DMA((LAYERS,)),
        ] + [pair] * 10 + [pltpu.SemaphoreType.DMA((2, RAW))] * 8,
        compiler_params=pltpu.CompilerParams(
            collective_id=0, has_side_effects=True, vmem_limit_bytes=56 * 1024 * 1024
        ),
        cost_estimate=pl.CostEstimate(
            flops=2 * rows * depth * width * 9, bytes_accessed=9 * 2 * depth * width,
            transcendentals=3 * rows * width),
    )(bins_in, pre_scale, pre_shift, conv_weight, conv_bias)


def solution(mesh):
    return jax.shard_map(
        functools.partial(per_device, mesh.shape["seq"]),
        mesh=mesh,
        in_specs=(
            P("seq", "ch"),
            P(None, "ch"),
            P(None, "ch"),
            P(None, None, None, "ch"),
            P(None, "ch"),
        ),
        out_specs=P("seq", "ch"),
        check_vma=False,
    )
```
